32 devices in a mesh: mem: 4 (over x, core), wide: 8 (over z, y).
Axes of the slice: x: 2, y: 2, z: 4, core: 2. Of those that a mesh axis runs over, the one named last changes fastest.
Arguments:
- control: float32 [8, 64, 128, 720], P('mem', 'wide'), may hold values from -6 to 6
- perturb: float32 [8, 3, 64, 128, 720], P('mem', None, None, 'wide'), may hold values from -6 to 6
- obs_count: int32 [128, 720], P('wide'), may hold values from 0 to 3
- obs_kind: int32 [128, 720], P('wide'), may hold values from 0 to 7
- obs_table: float32 [8, 192], replicated, may hold values from 0.25 to 4
- band_filter: float32 [64, 64], replicated, may hold values from -0.9 to 1.2, as said below
- diffusivity: float32 [128, 720], replicated, may hold values from 0.04 to 0.24
Outputs:
- hessian_product: float32 [8, 64, 128, 720], P('mem', 'wide')
The draws below stay inside these ranges and needn't reach their ends.
Inputs may be any that keep to these rules, and one draw needn't show every extreme that they name: band_filter[i, j] is zero where |i - j| > 4; its diagonal lies between 0.8 and 1.2.
All inputs are finite; a program needn't handle non-finite values.
Results may differ from the reference program's by a relative error of at most 0.00005.
Values sent between devices are 32-bit elements; how exact they have to be, the bound alone decides.
A program may use at most 128 MiB of HBM per device.

```python
import math
import jax
import jax.numpy as jnp
from jax import lax

LEVELS = 64
NLAT = 128
NLON = 720
ITERS = 16
HB = 4
KINDS = 8
MEMBERS = 8


def draw_band_filter(key, part):
    row_index = lax.broadcasted_iota(jnp.int32, (LEVELS, LEVELS), 0)
    col_index = lax.broadcasted_iota(jnp.int32, (LEVELS, LEVELS), 1)
    in_band = jnp.abs(row_index - col_index) <= HB
    key_off = jax.random.fold_in(key, 11)
    key_diag = jax.random.fold_in(key, 23)
    off_band = jnp.clip(0.3 * jax.random.normal(key_off, (LEVELS, LEVELS), jnp.float32), -0.9, 0.9)
    diagonal = jax.random.uniform(key_diag, (LEVELS, LEVELS), jnp.float32, 0.8, 1.2)
    return jnp.where(row_index == col_index, diagonal, jnp.where(in_band, off_band, jnp.zeros_like(off_band)))


def with_ends(result, stream_key, low, top_value):
    place = [jax.random.randint(jax.random.fold_in(stream_key, axis), (), 0, length) for axis, length in enumerate(result.shape)]
    main_axis = result.shape.index(max(result.shape))
    neighbour = place[:main_axis] + [(place[main_axis] + 1) % result.shape[main_axis]] + place[main_axis + 1:]
    return result.at[tuple(place)].set(low).at[tuple(neighbour)].set(top_value)


def block_scale(own_key, extent, shards, least, largest):
    def one(axis_at, shards_of):
        steps = jax.random.uniform(jax.random.fold_in(jax.random.fold_in(own_key, 6), axis_at), (shards_of,), jnp.float32, least / len(shards), largest / len(shards))
        return jnp.repeat(jnp.exp(steps), extent[axis_at] // shards_of).reshape((-1,) + (1,) * (len(extent) - axis_at - 1))

    loudness = one(*shards[0])
    for cut in shards[1:]:
        loudness = loudness * one(*cut)
    return loudness


def normal_values(rng, shape, width, limit, split=(), dtype=jnp.bfloat16):
    level = block_scale(rng, shape, split, -0.22, 0.18) if split else 1.0
    values = jax.random.normal(rng, shape, jnp.float32) * width * level
    return jnp.minimum(jnp.maximum(values, -limit), limit).astype(dtype)


def setup_inputs(seed: int = 0) -> dict:
    keys = jax.random.split(jax.random.key(seed), 8)
    return {
        "control": normal_values(keys[0], (MEMBERS, LEVELS, NLAT, NLON), 1.0, 6.0, ((0, 4), (1, 8)), jnp.float32),
        "perturb": normal_values(keys[1], (MEMBERS, 3, LEVELS, NLAT, NLON), 1.0, 6.0, ((0, 4), (3, 8)), jnp.float32),
        "obs_count": with_ends(jax.random.randint(keys[2], (NLAT, NLON), 0, 4), jax.random.fold_in(keys[2], 1), 0, 3).astype(jnp.int32),
        "obs_kind": with_ends(jax.random.randint(keys[3], (NLAT, NLON), 0, KINDS), jax.random.fold_in(keys[3], 1), 0, KINDS - 1).astype(jnp.int32),
        "obs_table": jnp.clip(jnp.exp(jax.random.uniform(keys[4], (KINDS, 3 * LEVELS), jnp.float32, math.log(0.25), math.log(4.0))), 0.25, 4.0),
        "band_filter": draw_band_filter(jax.random.fold_in(keys[7], 71), 0),
        "diffusivity": jnp.clip(jax.random.uniform(keys[6], (NLAT, NLON), jnp.float32, 0.04, 0.24), 0.04, 0.24),
    }


def edge_coeffs(diffusivity):
    east_edge = 0.5 * (diffusivity + jnp.roll(diffusivity, -1, axis=1))
    north_edge = 0.5 * (diffusivity + jnp.roll(diffusivity, -1, axis=0))
    row_index = lax.broadcasted_iota(jnp.int32, diffusivity.shape, 0)
    north_edge = jnp.where(row_index < diffusivity.shape[0] - 1, north_edge, jnp.zeros_like(north_edge))
    return east_edge, north_edge


def diffuse(field, east_edge, north_edge):
    def one_step(step_index, field_now):
        flux_east = east_edge * (jnp.roll(field_now, -1, axis=-1) - field_now)
        flux_north = north_edge * (jnp.roll(field_now, -1, axis=-2) - field_now)
        increment_field = flux_east - jnp.roll(flux_east, 1, axis=-1) + flux_north - jnp.roll(flux_north, 1, axis=-2)
        return field_now + increment_field
    return lax.fori_loop(0, ITERS, one_step, field)


def reference(control, perturb, obs_count, obs_kind, obs_table, band_filter, diffusivity):
    highest_level = lax.Precision.HIGHEST
    east_edge, north_edge = edge_coeffs(diffusivity)
    smooth = diffuse(control, east_edge, north_edge)
    filtered_field = jnp.einsum("lm,kmij->klij", band_filter, smooth, precision=highest_level)
    increment_field = jnp.einsum("kvlij,klij->vlij", perturb, filtered_field, precision=highest_level)
    looked_up = obs_table[obs_kind].reshape(NLAT, NLON, 3, LEVELS)
    weights = jnp.transpose(looked_up, (2, 3, 0, 1)) * obs_count.astype(jnp.float32)[None, None, :, :]
    weighted_field = weights * increment_field
    adjoint_field = jnp.einsum("kvlij,vlij->klij", perturb, weighted_field, precision=highest_level)
    lifted = jnp.einsum("lm,klij->kmij", band_filter, adjoint_field, precision=highest_level)
    return control + diffuse(lifted, east_edge, north_edge)
```

```python
import functools

import jax
import jax.numpy as jnp
from jax import lax
from jax.experimental import pallas as pl
from jax.experimental.pallas import tpu as pltpu
from jax.sharding import PartitionSpec as P

ITERS = 16
HB = 4
LANES = 128
VMEM_LIMIT = 48 * 1024 * 1024


def edge_coeffs(diffusivity):
    east_edge = 0.5 * (diffusivity + jnp.roll(diffusivity, -1, axis=1))
    north_edge = 0.5 * (diffusivity + jnp.roll(diffusivity, -1, axis=0))
    row_index = lax.broadcasted_iota(jnp.int32, diffusivity.shape, 0)
    north_edge = jnp.where(
        row_index < diffusivity.shape[0] - 1, north_edge, jnp.zeros_like(north_edge)
    )
    return (east_edge, north_edge)


def strip_rows(count):
    return 8 if count % 8 == 0 else count


def run_steps(nlon, scr, east_ref, north_ref):
    rows = strip_rows(nlon)
    strips = nlon // rows
    nlat = scr.shape[1]
    row_index = lax.broadcasted_iota(jnp.int32, (rows, nlat), 0)
    is_last = row_index == rows - 1
    is_first = row_index == 0

    def one_step(_, carry):
        cur = scr[pl.ds(0, rows), :]
        rot_first = rot_cur = pltpu.roll(cur, rows - 1, 0)
        end = pl.ds((strips - 1) * rows, rows)
        last = scr[end, :]
        beyond = jnp.where(is_last, rot_first, pltpu.roll(last, rows - 1, 0))
        rot_fe_prev = pltpu.roll(east_ref[end, :] * (beyond - last), 1, 0)
        for strip in range(strips):
            here = pl.ds(strip * rows, rows)
            if strip < strips - 1:
                nxt = scr[pl.ds((strip + 1) * rows, rows), :]
                rot_nxt = pltpu.roll(nxt, rows - 1, 0)
            else:
                nxt, rot_nxt = cur, rot_first
            flux_east = east_ref[here, :] * (jnp.where(is_last, rot_nxt, rot_cur) - cur)
            rot_fe = pltpu.roll(flux_east, 1, 0)
            flux_west = jnp.where(is_first, rot_fe_prev, rot_fe)
            flux_north = north_ref[here, :] * (pltpu.roll(cur, nlat - 1, 1) - cur)
            flux_south = pltpu.roll(flux_north, 1, 1)
            scr[here, :] = cur + (flux_east - flux_west + flux_north - flux_south)
            cur, rot_cur, rot_fe_prev = nxt, rot_nxt, rot_fe
        return carry

    lax.fori_loop(0, ITERS, one_step, 0)


def forward_kernel(bounds, chunk, east_ref, north_ref, control_ref, *rest):
    outs, scr = rest[:-1], rest[-1]
    nlon = control_ref.shape[2]
    scr[pl.ds(0, nlon), :] = control_ref[0, 0]
    if scr.shape[0] > nlon:
        scr[pl.ds(nlon, scr.shape[0] - nlon), :] = jnp.zeros(
            (scr.shape[0] - nlon, scr.shape[1]), jnp.float32
        )
    run_steps(nlon, scr, east_ref, north_ref)
    for (start, stop), out in zip(bounds, outs):
        per = out.shape[3]
        turned = scr[pl.ds(start, chunk), :].T
        for dest in range(out.shape[0]):
            out[dest, 0, 0] = turned[dest * per : (dest + 1) * per, : stop - start]


def backward_kernel(bounds, east_ref, north_ref, control_ref, *rest):
    parts, out_ref, scr, turn = rest[:-3], rest[-3], rest[-2], rest[-1]
    nlon = out_ref.shape[2]
    for (start, stop), part in zip(bounds, parts):
        per = part.shape[3]
        for source in range(part.shape[0]):
            turn[pl.ds(source * per, per), pl.ds(0, stop - start)] = part[source, 0, 0]
        scr[pl.ds(start, stop - start), :] = turn[...].T[: stop - start]
    run_steps(nlon, scr, east_ref, north_ref)
    out_ref[0, 0] = control_ref[0, 0] + scr[pl.ds(0, nlon), :]


def window(level, levels):
    return range(max(0, level - HB), min(levels, level + HB + 1))


def increment_kernel(levels, smooth_ref, perturb_ref, band_ref, flag_ref, keep_ref, give_ref):
    mem_dev, variables = perturb_ref.shape[:2]
    per = smooth_ref.shape[2]
    lower_mine = jnp.full(perturb_ref.shape[3:], flag_ref[0], jnp.int32) == 0
    half = levels // 2

    def partial_sums(level):
        filtered = []
        for member in range(mem_dev):
            total = None
            for m in window(level, levels):
                term = band_ref[level, m] * smooth_ref[m // per, member, m % per]
                total = term if total is None else total + term
            filtered.append(total)
        sums = []
        for variable in range(variables):
            total = perturb_ref[0, variable, level] * filtered[0]
            for member in range(1, mem_dev):
                total = total + perturb_ref[member, variable, level] * filtered[member]
            sums.append(total)
        return sums

    for row in range(half):
        lower, upper = partial_sums(row), partial_sums(row + half)
        for variable in range(variables):
            keep_ref[variable, row] = jnp.where(lower_mine, lower[variable], upper[variable])
            give_ref[variable, row] = jnp.where(lower_mine, upper[variable], lower[variable])


def adjoint_kernel(
    levels, mine_ref, other_ref, perturb_ref, count_ref, kind_ref, flag_ref, table_ref, band_ref, out_ref
):
    mem_dev, variables = perturb_ref.shape[:2]
    per = out_ref.shape[2]
    half = levels // 2
    count = count_ref[...].astype(jnp.float32)
    kind = kind_ref[...]
    kinds = table_ref.shape[0]
    masks = [kind == q for q in range(kinds)]
    lower_mine = jnp.full(kind.shape, flag_ref[0], jnp.int32) == 0
    adjoint = {}
    for step in range(levels + HB):
        if step < levels:
            weighted = []
            for variable in range(variables):
                column = variable * levels + step
                looked_up = jnp.full(kind.shape, table_ref[0, column], jnp.float32)
                for q in range(1, kinds):
                    looked_up = jnp.where(masks[q], table_ref[q, column], looked_up)
                mine, other = mine_ref[variable, step % half], other_ref[variable, step % half]
                if step < half:
                    increment = jnp.where(lower_mine, mine, other)
                else:
                    increment = jnp.where(lower_mine, other, mine)
                weighted.append(looked_up * count * increment)
            for member in range(mem_dev):
                total = perturb_ref[member, 0, step] * weighted[0]
                for variable in range(1, variables):
                    total = total + perturb_ref[member, variable, step] * weighted[variable]
                adjoint[member, step] = total
        m = step - HB
        if m >= 0:
            for member in range(mem_dev):
                total = None
                for level in window(m, levels):
                    term = band_ref[level, m] * adjoint[member, level]
                    total = term if total is None else total + term
                out_ref[m // per, member, m % per] = total


def member_sum(devices, keep, give):
    cores = [(d, d ^ 1) for d in range(devices)]
    mine = keep + lax.ppermute(give, "mem", cores)
    pairs = mine
    for shift in range(1, devices // 2):
        step = [(d, (d + 2 * shift) % devices) for d in range(devices)]
        mine = mine + lax.ppermute(pairs, "mem", step)
    return mine, lax.ppermute(mine, "mem", cores)


def local(wide, members, control, perturb, obs_count, obs_kind, obs_table, band_filter, diffusivity):
    mem_dev, lev_dev, nlat, nlon = control.shape
    variables, levels, lat_dev = perturb.shape[1:4]
    east_edge, north_edge = edge_coeffs(diffusivity)
    east_edge, north_edge = east_edge.T, north_edge.T
    control = jnp.swapaxes(control, 2, 3)
    chunk = 2 * LANES
    bounds = [(start, min(start + chunk, nlon)) for start in range(0, nlon, chunk)]
    params = pltpu.CompilerParams(vmem_limit_bytes=VMEM_LIMIT)
    whole = pl.BlockSpec((nlon, nlat), lambda k, l: (0, 0))
    plane = pl.BlockSpec((1, 1, nlon, nlat), lambda k, l: (k, l, 0, 0))
    pieces = [
        pl.BlockSpec((wide, 1, 1, lat_dev, stop - start), lambda k, l: (0, k, l, 0, 0))
        for start, stop in bounds
    ]
    piece_shapes = [
        jax.ShapeDtypeStruct((wide, mem_dev, lev_dev, lat_dev, stop - start), jnp.float32)
        for start, stop in bounds
    ]
    field_bytes = 4 * mem_dev * lev_dev * nlat * nlon
    steps_cost = pl.CostEstimate(
        flops=ITERS * 9 * field_bytes // 4, bytes_accessed=2 * field_bytes, transcendentals=0
    )
    smooth = pl.pallas_call(
        functools.partial(forward_kernel, bounds, chunk),
        grid=(mem_dev, lev_dev),
        in_specs=[whole, whole, plane],
        out_specs=pieces,
        out_shape=piece_shapes,
        scratch_shapes=[pltpu.VMEM((len(bounds) * chunk, nlat), jnp.float32)],
        compiler_params=params,
        cost_estimate=steps_cost,
    )(east_edge, north_edge, control)

    tile = strip_rows(lat_dev)
    smem = pl.BlockSpec(memory_space=pltpu.SMEM)
    flag = (lax.axis_index("mem") % 2).reshape((1,)).astype(jnp.int32)
    moved = []
    for (start, stop), part in zip(bounds, smooth):
        columns = lax.all_to_all(part, "wide", split_axis=0, concat_axis=0)
        size = stop - start
        first = start // LANES
        grid = (lat_dev // tile, -(-size // LANES))
        column_spec = pl.BlockSpec(
            (wide, mem_dev, lev_dev, tile, LANES), lambda i, j: (0, 0, 0, i, j)
        )
        perturb_spec = pl.BlockSpec(
            (mem_dev, variables, levels, tile, LANES),
            lambda i, j, first=first: (0, 0, 0, i, first + j),
        )
        half_spec = pl.BlockSpec((variables, levels // 2, tile, LANES), lambda i, j: (0, 0, i, j))
        half_shape = jax.ShapeDtypeStruct((variables, levels // 2, lat_dev, size), jnp.float32)
        cell_spec = pl.BlockSpec((tile, LANES), lambda i, j, first=first: (i, first + j))
        cells = lat_dev * size * levels
        cost = pl.CostEstimate(
            flops=cells * 60, bytes_accessed=4 * cells * (mem_dev * 4 + 3), transcendentals=0
        )
        keep, give = pl.pallas_call(
            functools.partial(increment_kernel, levels),
            grid=grid,
            in_specs=[column_spec, perturb_spec, smem, smem],
            out_specs=[half_spec, half_spec],
            out_shape=[half_shape, half_shape],
            compiler_params=params,
            cost_estimate=cost,
        )(columns, perturb, band_filter, flag)
        mine, other = member_sum(members, keep, give)
        lifted = pl.pallas_call(
            functools.partial(adjoint_kernel, levels),
            grid=grid,
            in_specs=[half_spec, half_spec, perturb_spec, cell_spec, cell_spec, smem, smem, smem],
            out_specs=column_spec,
            out_shape=jax.ShapeDtypeStruct((wide, mem_dev, lev_dev, lat_dev, size), jnp.float32),
            compiler_params=params,
            cost_estimate=cost,
        )(mine, other, perturb, obs_count, obs_kind, flag, obs_table, band_filter)
        moved.append(lax.all_to_all(lifted, "wide", split_axis=0, concat_axis=0))

    product = pl.pallas_call(
        functools.partial(backward_kernel, bounds),
        grid=(mem_dev, lev_dev),
        in_specs=[whole, whole, plane] + pieces,
        out_specs=plane,
        out_shape=jax.ShapeDtypeStruct(control.shape, jnp.float32),
        scratch_shapes=[
            pltpu.VMEM((nlon, nlat), jnp.float32),
            pltpu.VMEM((nlat, chunk), jnp.float32),
        ],
        compiler_params=params,
        cost_estimate=steps_cost,
    )(east_edge, north_edge, control, *moved)
    return jnp.swapaxes(product, 2, 3)


def solution(mesh):
    placed = (
        P("mem", "wide", None, None),
        P("mem", None, None, "wide", None),
        P("wide", None),
        P("wide", None),
        P(),
        P(),
        P(),
    )
    return jax.shard_map(
        functools.partial(local, mesh.shape["wide"], mesh.shape["mem"]),
        mesh=mesh,
        in_specs=placed,
        out_specs=P("mem", "wide", None, None),
        check_vma=False,
    )
```
